256 devices in a mesh: pts: 16 (over z, core), trc: 16 (over y, x).
Axes of the slice: x: 4, y: 4, z: 8, core: 2. Of those that a mesh axis runs over, the one named last changes fastest.
Arguments:
- tracers: float32 [64, 49152], P('trc', 'pts'), may hold values from -6 to 6
- explicit_blocks: bfloat16 [2, 384, 4, 128, 128], P(None, 'pts'), may hold values from -0.375 to 0.375
- implicit_blocks: bfloat16 [2, 384, 4, 128, 128], P(None, 'pts'), may hold values from -0.375 to 0.375
- column_blocks: int32 [384, 4], P('pts'), may hold values from 0 to 383, as said below
- block_count: int32 [384], P('pts'), may hold values from 1 to 4
- month_pair: int32 [2], replicated, may hold values from 0 to 1, as said below
- weight_num: int32 [2], replicated, may hold values from 0 to 30
- source_mix: float32 [64, 64], replicated, may hold values from -0.75 to 0.75
- source_bias: float32 [64], replicated, may hold values from -3 to 3
- source_rate: float32 [64], replicated, may hold values from 0.2 to 2
Outputs:
- advanced: float32 [64, 49152], P('trc', 'pts')
The draws below stay inside these ranges and needn't reach their ends.
Inputs may be any that keep to these rules, and one draw needn't show every extreme that they name: `month_pair`: the two months differ. column_blocks[n, r] = (n + d) mod 384 with -2 <= d < 2, the entries of one row-block distinct.
All inputs are finite; a program needn't handle non-finite values.
Results may differ from the reference program's by a relative error of at most 0.0003.
Values sent between devices are 32-bit elements; how exact they have to be, the bound alone decides.
No kernel may reach another device: no remote copies, remote signals or barrier semaphores. Data moves between devices by JAX's collectives and lax.ppermute only.
A program may use at most 64 MiB of HBM per device.

```python
import math
import jax
import jax.numpy as jnp
from jax import lax

TR = 64
BS = 128
R = 4
REACH = 2
MONTHS = 2
DAYS = 30
STEPS = 2
NB = 384
NPTS = 49152


def draw_month_pair(key, part):
    first = jax.random.randint(key, (1,), 0, 2)
    return jnp.concatenate([first, 1 - first]).astype(jnp.int32)


def draw_column_blocks(key, part):
    row_keys = jax.random.split(key, NB)
    chosen = jax.vmap(lambda k: jax.random.permutation(k, 2 * REACH))(row_keys)[:, :R]
    offsets = chosen.astype(jnp.int32) - REACH
    rows = jnp.arange(NB, dtype=jnp.int32)[:, None]
    return ((rows + offsets) % NB).astype(jnp.int32)


def set_ends(array, key, least, high):
    longest = array.shape.index(max(array.shape))
    spots = []
    for shift in (0, 1):
        where = [jax.random.randint(jax.random.fold_in(key, axis), (), 0, length) for axis, length in enumerate(array.shape)]
        where[longest] = (where[longest] + shift) % array.shape[longest]
        spots.append(tuple(where))
    return array.at[spots[0]].set(least).at[spots[1]].set(high)


def levels(key, dims, shards, smallest, high):
    factor_of = 1.0
    for axis_at, parts in shards:
        heights = jax.random.uniform(jax.random.fold_in(jax.random.fold_in(key, 6), axis_at), (parts,), jnp.float32, smallest / len(shards), high / len(shards))
        factor_of = factor_of * jnp.repeat(jnp.exp(heights), dims[axis_at] // parts).reshape((-1,) + (1,) * (len(dims) - 1 - axis_at))
    return factor_of


def normal_values(key, shape, spread, limit, cuts=(), kind=jnp.bfloat16):
    level = levels(key, shape, cuts, -0.22, 0.18) if cuts else 1.0
    array = jax.random.normal(key, shape, jnp.float32) * spread * level
    return jnp.minimum(jnp.maximum(array, -limit), limit).astype(kind)


def setup_inputs(seed: int = 0) -> dict:
    arg_keys = jax.random.split(jax.random.key(seed), 11)
    tracers = normal_values(arg_keys[0], (TR, NPTS), 1.0, 6.0, ((0, 16), (1, 16)), jnp.float32)
    explicit_blocks = normal_values(arg_keys[1], (MONTHS, NB, R, BS, BS), (R * BS // 2) ** -0.5, 0.375, ((1, 16),))
    implicit_blocks = normal_values(arg_keys[2], (MONTHS, NB, R, BS, BS), (R * BS // 2) ** -0.5, 0.375, ((1, 16),))
    column_blocks = draw_column_blocks(jax.random.fold_in(arg_keys[10], 71), 0)
    block_count = set_ends(jax.random.randint(arg_keys[4], (NB,), 1, R + 1), jax.random.fold_in(arg_keys[4], 1), 1, R).astype(jnp.int32)
    month_pair = draw_month_pair(jax.random.fold_in(arg_keys[10], 71), 0)
    weight_num = jax.random.randint(arg_keys[6], (STEPS,), 0, DAYS + 1).astype(jnp.int32)
    source_mix = normal_values(arg_keys[7], (TR, TR), TR ** -0.5, 0.75, (), jnp.float32)
    source_bias = normal_values(arg_keys[8], (TR,), 0.5, 3.0, (), jnp.float32)
    source_rate = jnp.clip(jnp.exp(jax.random.uniform(arg_keys[9], (TR,), jnp.float32, math.log(0.2), math.log(2.0))), 0.2, 2.0)
    return {"tracers": tracers, "explicit_blocks": explicit_blocks, "implicit_blocks": implicit_blocks, "column_blocks": column_blocks, "block_count": block_count, "month_pair": month_pair, "weight_num": weight_num, "source_mix": source_mix, "source_bias": source_bias, "source_rate": source_rate}


def interpolate(blocks, month_pair, numer):
    first = lax.dynamic_index_in_dim(blocks, month_pair[0], 0, keepdims=False).astype(jnp.float32)
    second = lax.dynamic_index_in_dim(blocks, month_pair[1], 0, keepdims=False).astype(jnp.float32)
    weight = numer.astype(jnp.float32) / DAYS
    return (1.0 - weight) * first + weight * second


def apply_op(matrix, column_blocks, block_count, field):
    split = field.reshape(TR, NB, BS)
    picked = split[:, column_blocks]
    used = (jnp.arange(R)[None, :] < block_count[:, None]).astype(jnp.float32)
    picked = picked * used[None, :, :, None]
    out = jnp.einsum("nrij,tnrj->tni", matrix, picked, precision=lax.Precision.HIGHEST)
    return out.reshape(TR, NPTS)


def source(field, source_mix, source_bias, source_rate):
    inner = jnp.dot(source_mix, field, precision=lax.Precision.HIGHEST) + source_bias[:, None]
    return source_rate[:, None] * inner * jnp.exp(-0.125 * inner * inner)


def reference(tracers, explicit_blocks, implicit_blocks, column_blocks, block_count, month_pair, weight_num, source_mix, source_bias, source_rate):
    field = tracers
    for step in range(STEPS):
        explicit_op = interpolate(explicit_blocks, month_pair, weight_num[step])
        implicit_op = interpolate(implicit_blocks, month_pair, weight_num[step])
        middle = apply_op(explicit_op, column_blocks, block_count, field) + 0.5 * source(field, source_mix, source_bias, source_rate)
        field = apply_op(implicit_op, column_blocks, block_count, middle)
    return field
```

```python
import jax
import jax.numpy as jnp
from jax import lax
from jax.experimental import pallas as pl
from jax.experimental.pallas import tpu as pltpu
from jax.sharding import PartitionSpec as P

REACH = 2
DAYS = 30
STEPS = 2
LOW = 2 * REACH
HIGH = 2 * (REACH - 1)
F32 = jnp.float32
BF16 = jnp.bfloat16
MIB = 1 << 20
NT = (((1,), (1,)), ((), ()))


def split_store(ref, where, value):
    half = value.shape[0]
    high = value.astype(BF16)
    ref[where, 0:half, :] = high
    ref[where, half : 2 * half, :] = (value - high.astype(F32)).astype(BF16)


def combine(product, coef_ref, step):
    block = product.shape[1] // 2
    half = product.shape[0] // 2
    mixed = coef_ref[step, 0] * product[:, :block] + coef_ref[step, 1] * product[:, block:]
    return mixed[:half] + mixed[half:]


def own_row(values_ref, blocks_ref, cols_ref, row, shift, coef_ref, step):
    width = blocks_ref.shape[2]
    left = jnp.concatenate([values_ref[cols_ref[row, r] - shift] for r in range(width)], axis=1)
    right = jnp.concatenate(
        [
            jnp.concatenate([blocks_ref[m, row, r] for r in range(width)], axis=1)
            for m in range(2)
        ],
        axis=0,
    )
    product = lax.dot_general(left, right, NT, preferred_element_type=F32)
    return combine(product, coef_ref, step)


def edge_row(values_ref, edge_ref, row, first, coef_ref, step):
    width = edge_ref.shape[2]
    left = jnp.concatenate([values_ref[first + d] for d in range(width)], axis=1)
    right = jnp.concatenate(
        [
            jnp.concatenate([edge_ref[m, row, d].astype(BF16) for d in range(width)], axis=1)
            for m in range(2)
        ],
        axis=0,
    )
    product = lax.dot_general(left, right, NT, preferred_element_type=F32)
    return combine(product, coef_ref, step)


def mixing_tile(mix_ref):
    mix = mix_ref[...]
    high = mix.astype(BF16)
    low = (mix - high.astype(F32)).astype(BF16)
    return jnp.concatenate([high, low], axis=0)


def half_source(values, mixing, bias_ref, rate_ref):
    both = lax.dot_general(
        mixing, values, (((1,), (0,)), ((), ())), preferred_element_type=F32
    )
    half = both.shape[0] // 2
    inner = both[:half] + both[half:] + bias_ref[...]
    return rate_ref[...] * inner * jnp.exp(-0.125 * inner * inner)


def edges_kernel(position_ref, cols_ref, low_ref, high_ref, to_right_ref, to_left_ref):
    reach_cols = low_ref.shape[2]
    for source_ref, target_ref, start in (
        (low_ref, to_right_ref, position_ref[0]),
        (high_ref, to_left_ref, 0),
    ):
        for row in range(source_ref.shape[1]):
            n = start + row
            for d in range(reach_cols):
                wanted = n + LOW - REACH + d
                slot = jnp.int32(0)
                scale = jnp.float32(0.0)
                for r in range(reach_cols):
                    hit = cols_ref[n, r] == wanted
                    slot = jnp.where(hit, r, slot)
                    scale = jnp.where(hit, 1.0, scale)
                for m in range(2):
                    target_ref[m, row, d] = source_ref[m, row, slot].astype(F32) * scale


def pack_edges(explicit_blocks, cols):
    months, rows, width, block, _ = explicit_blocks.shape
    spec = lambda count, at: pl.BlockSpec(
        (months, count, width, block, block), lambda i: (0, at, 0, 0, 0)
    )
    smem = pl.BlockSpec(memory_space=pltpu.SMEM)
    shape = lambda count: jax.ShapeDtypeStruct((months, count, width, block, block), F32)
    return pl.pallas_call(
        edges_kernel,
        grid=(1,),
        in_specs=[
            smem,
            smem,
            spec(REACH, rows // REACH - 1),
            spec(REACH - 1, 0),
        ],
        out_specs=[spec(REACH, 0), spec(REACH - 1, 0)],
        out_shape=[shape(REACH), shape(REACH - 1)],
        name="edges",
    )(jnp.full((1,), rows - REACH, jnp.int32), cols, explicit_blocks, explicit_blocks)


def first_kernel(
    cols_ref, coef_ref, field_ref, explicit_ref, implicit_ref, left_ref, right_ref,
    mix_ref, bias_ref, rate_ref, low_ref, high_ref, field_out_ref, values_ref, middle_ref,
):
    rows = explicit_ref.shape[1]
    block = explicit_ref.shape[-1]
    tracers = mix_ref.shape[0]
    ext = rows + LOW + HIGH
    zero = jnp.zeros((2 * tracers, block), BF16)
    values_ref[ext] = zero
    middle_ref[ext - REACH] = zero
    for b in range(ext):
        split_store(values_ref, b, field_ref[pl.ds(b, tracers, stride=ext), :])
    mixing = mixing_tile(mix_ref)

    def finish(frame, product):
        source = half_source(values_ref[frame + REACH], mixing, bias_ref, rate_ref)
        split_store(middle_ref, frame, product + source)

    for row in range(REACH):
        finish(row, edge_row(values_ref, left_ref, row, row, coef_ref, 0))
    for row in range(REACH - 1):
        frame = rows + REACH + row
        finish(frame, edge_row(values_ref, right_ref, row, frame, coef_ref, 0))

    def explicit_row(row, carry):
        finish(row + REACH, own_row(values_ref, explicit_ref, cols_ref, row, 0, coef_ref, 0))
        return carry

    lax.fori_loop(0, rows, explicit_row, 0, unroll=4)

    for row in range(LOW):
        result = own_row(
            middle_ref, implicit_ref, cols_ref, rows - LOW + row, REACH, coef_ref, 0
        )
        low_ref[:, row * block : (row + 1) * block] = result
        split_store(field_out_ref, rows - LOW + row, result)
    for row in range(HIGH):
        result = own_row(middle_ref, implicit_ref, cols_ref, row, REACH, coef_ref, 0)
        high_ref[:, row * block : (row + 1) * block] = result
        split_store(field_out_ref, row, result)

    def implicit_row(row, carry):
        split_store(
            field_out_ref,
            row,
            own_row(middle_ref, implicit_ref, cols_ref, row, REACH, coef_ref, 0),
        )
        return carry

    lax.fori_loop(HIGH, rows - LOW, implicit_row, 0, unroll=3)


def inner_kernel(
    cols_ref, coef_ref, field_ref, explicit_ref, mix_ref, bias_ref, rate_ref,
    middle_ref, values_ref,
):
    rows = explicit_ref.shape[1]
    values_ref[LOW : LOW + rows] = field_ref[...]
    values_ref[rows + LOW + HIGH] = jnp.zeros(values_ref.shape[1:], BF16)
    mixing = mixing_tile(mix_ref)

    def explicit_row(row, carry):
        product = own_row(values_ref, explicit_ref, cols_ref, row, 0, coef_ref, 1)
        source = half_source(values_ref[row + LOW], mixing, bias_ref, rate_ref)
        split_store(middle_ref, row, product + source)
        return carry

    lax.fori_loop(REACH, rows - REACH + 1, explicit_row, 0, unroll=3)


def last_kernel(
    cols_ref, coef_ref, place_ref, low_in_ref, high_in_ref, field_ref, middle_in_ref,
    explicit_ref, implicit_ref, left_ref, right_ref, mix_ref, bias_ref, rate_ref,
    out_ref, values_ref, middle_ref, result_ref,
):
    rows = explicit_ref.shape[1]
    block = explicit_ref.shape[-1]
    tracers = mix_ref.shape[0]
    ext = rows + LOW + HIGH
    zero = jnp.zeros((2 * tracers, block), BF16)
    values_ref[ext] = zero
    middle_ref[ext - REACH] = zero
    values_ref[LOW : LOW + rows] = field_ref[...]
    middle_ref[2 * REACH : rows + 1] = middle_in_ref[REACH : rows - REACH + 1]
    for b in range(LOW):
        split_store(values_ref, b, low_in_ref[:, b * block : (b + 1) * block])
    for b in range(HIGH):
        split_store(values_ref, LOW + rows + b, high_in_ref[:, b * block : (b + 1) * block])
    mixing = mixing_tile(mix_ref)

    def finish(frame, product):
        source = half_source(values_ref[frame + REACH], mixing, bias_ref, rate_ref)
        split_store(middle_ref, frame, product + source)

    for row in range(REACH):
        finish(row, edge_row(values_ref, left_ref, row, row, coef_ref, 1))
    for row in range(REACH - 1):
        frame = rows + REACH + row
        finish(frame, edge_row(values_ref, right_ref, row, frame, coef_ref, 1))
    for row in [*range(REACH), *range(rows - REACH + 1, rows)]:
        finish(row + REACH, own_row(values_ref, explicit_ref, cols_ref, row, 0, coef_ref, 1))

    for row in range(rows):
        result_ref[:, row * block : (row + 1) * block] = own_row(
            middle_ref, implicit_ref, cols_ref, row, REACH, coef_ref, 1
        )
    mine = out_ref.shape[0]
    place = place_ref[0]
    pair = result_ref[pl.ds(pl.multiple_of((place // 2) * 2 * mine, 2 * mine), 2 * mine), :]
    out_ref[...] = jnp.where(place % 2 == 0, pair[:mine], pair[mine:])


def call(kernel, name, smem_count, args, outs, scratch, flops, limit):
    smem = pl.BlockSpec(memory_space=pltpu.SMEM)
    vmem = pl.BlockSpec(memory_space=pltpu.VMEM)
    return pl.pallas_call(
        kernel,
        in_specs=[smem] * smem_count + [vmem] * (len(args) - smem_count),
        out_specs=[vmem] * len(outs),
        out_shape=outs,
        scratch_shapes=scratch,
        compiler_params=pltpu.CompilerParams(vmem_limit_bytes=limit * MIB),
        cost_estimate=pl.CostEstimate(flops=flops, bytes_accessed=8 * MIB, transcendentals=0),
        name=name,
    )(*args)


def per_device(
    tracers,
    explicit_blocks,
    implicit_blocks,
    column_blocks,
    block_count,
    month_pair,
    weight_num,
    source_mix,
    source_bias,
    source_rate,
):
    rows, width = column_blocks.shape
    block = explicit_blocks.shape[-1]
    parts = lax.axis_size("pts")
    groups = lax.axis_size("trc")
    mine = tracers.shape[0]
    total = source_mix.shape[0]
    ext = rows + LOW + HIGH
    forward = [(i, (i + 1) % parts) for i in range(parts)]
    backward = [(target, source) for source, target in forward]

    used = jnp.arange(width)[None, :] < block_count[:, None]
    cols = (column_blocks - lax.axis_index("pts") * rows + LOW) % (rows * parts)
    cols = jnp.where(used, cols, ext).astype(jnp.int32)
    weight = weight_num.astype(F32) / DAYS
    straight = month_pair[0] == 0
    coef = jnp.stack(
        [jnp.where(straight, 1.0 - weight, weight), jnp.where(straight, weight, 1.0 - weight)],
        axis=1,
    )
    mix = jnp.concatenate([source_mix, source_mix], axis=1)
    bias = source_bias[:, None]
    rate = 0.5 * source_rate[:, None]
    place = lax.axis_index("trc").astype(jnp.int32).reshape(1)

    low = lax.ppermute(tracers[:, -LOW * block :], "pts", forward)
    high = lax.ppermute(tracers[:, : HIGH * block], "pts", backward)
    to_right, to_left = pack_edges(explicit_blocks, cols)
    extended = jnp.concatenate([low, tracers, high], axis=1)
    extended = extended.reshape(mine * ext, block)
    gathered = lax.all_to_all(
        jnp.broadcast_to(extended[None], (groups,) + extended.shape),
        "trc", split_axis=0, concat_axis=0, tiled=True,
    )
    gathered = gathered.reshape(total * ext, block)
    left = lax.ppermute(to_right, "pts", forward)
    right = lax.ppermute(to_left, "pts", backward)

    shape = jax.ShapeDtypeStruct
    stack = lambda count: pltpu.VMEM((count, 2 * total, block), BF16)
    one = 2 * 2 * total * 2 * block * width * block
    low, high, field = call(
        first_kernel, "first", 2,
        (cols, coef, gathered, explicit_blocks, implicit_blocks, left, right, mix, bias, rate),
        [
            shape((total, LOW * block), F32),
            shape((total, HIGH * block), F32),
            shape((rows, 2 * total, block), BF16),
        ],
        [stack(ext + 1), stack(ext - REACH + 1)],
        51 * one, 26,
    )
    low = lax.ppermute(low, "pts", forward)
    high = lax.ppermute(high, "pts", backward)
    (middle,) = call(
        inner_kernel, "inner", 2,
        (cols, coef, field, explicit_blocks, mix, bias, rate),
        [shape((rows, 2 * total, block), BF16)],
        [stack(ext + 1)],
        21 * one, 18,
    )
    (advanced,) = call(
        last_kernel, "last", 3,
        (
            cols, coef, place, low, high, field, middle, explicit_blocks, implicit_blocks,
            left, right, mix, bias, rate,
        ),
        [shape((mine, rows * block), F32)],
        [stack(ext + 1), stack(ext - REACH + 1), pltpu.VMEM((total, rows * block), F32)],
        30 * one, 26,
    )
    return advanced


def solution(mesh):
    in_specs = (
        P("trc", "pts"),
        P(None, "pts", None, None, None),
        P(None, "pts", None, None, None),
        P("pts", None),
        P("pts"),
        P(),
        P(),
        P(),
        P(),
        P(),
    )
    out_specs = P("trc", "pts")
    return jax.shard_map(
        per_device, mesh=mesh, in_specs=in_specs, out_specs=out_specs, check_vma=False
    )
```

```python
import functools

import jax
import jax.numpy as jnp
from jax import lax
from jax.experimental import pallas as pl
from jax.experimental.pallas import tpu as pltpu
from jax.sharding import PartitionSpec as P

REACH = 2
DAYS = 30
STEPS = 2
LOW = 2 * REACH
HIGH = 2 * (REACH - 1)
F32 = jnp.float32
BF16 = jnp.bfloat16
MIB = 1 << 20
SIDE = 4
NT = (((1,), (1,)), ((), ()))


def split_store(ref, where, value):
    half = value.shape[0]
    high = value.astype(BF16)
    ref[where, 0:half, :] = high
    ref[where, half : 2 * half, :] = (value - high.astype(F32)).astype(BF16)


def coefficients(month_ref, weight_ref, step):
    weight = weight_ref[step].astype(F32) * (1.0 / DAYS)
    straight = month_ref[0] == 0
    return (
        jnp.where(straight, 1.0 - weight, weight),
        jnp.where(straight, weight, 1.0 - weight),
    )


def combine(product, coef):
    block = product.shape[1] // 2
    half = product.shape[0] // 2
    mixed = coef[0] * product[:, :block] + coef[1] * product[:, block:]
    return mixed[:half] + mixed[half:]


def column(total, origin_ref, cols_ref, count_ref, row, r, spare):
    at = cols_ref[r, row] - origin_ref[0] * cols_ref.shape[1] + LOW
    at = jnp.where(at < 0, at + total, at)
    at = jnp.where(at >= total, at - total, at)
    return jnp.where(r < count_ref[row], at, spare)


def own_row(values_ref, blocks_ref, tables, row, shift, coef):
    width = blocks_ref.shape[2]
    spare = blocks_ref.shape[1] + LOW + HIGH
    left = jnp.concatenate(
        [values_ref[column(*tables, row, r, spare) - shift] for r in range(width)], axis=1
    )
    right = jnp.concatenate(
        [
            jnp.concatenate([blocks_ref[m, row, r] for r in range(width)], axis=1)
            for m in range(2)
        ],
        axis=0,
    )
    product = lax.dot_general(left, right, NT, preferred_element_type=F32)
    return combine(product, coef)


def edge_row(values_ref, edge_ref, row, first, coef):
    width = edge_ref.shape[2]
    left = jnp.concatenate([values_ref[first + d] for d in range(width)], axis=1)
    right = jnp.concatenate(
        [
            jnp.concatenate([edge_ref[m, row, d].astype(BF16) for d in range(width)], axis=1)
            for m in range(2)
        ],
        axis=0,
    )
    product = lax.dot_general(left, right, NT, preferred_element_type=F32)
    return combine(product, coef)


def prepare_source(side, part, place, mix_ref, bias_ref, rate_ref, mixing_ref, bias_out_ref, rate_out_ref):
    size = mix_ref.shape[0]
    mine = size // (side * side)
    at = lax.broadcasted_iota(jnp.int32, (size, size), 0)
    wanted = lax.broadcasted_iota(jnp.int32, (size, size), 1)
    outer, inner = at // (mine * side), lax.rem(at // mine, side)
    even = lax.rem(part, 2) == 0
    y = lax.rem(place // side + jnp.where(even, outer, inner), side)
    x = lax.rem(lax.rem(place, side) + jnp.where(even, inner, outer), side)
    chosen = (y * side + x) * mine + lax.rem(at, mine) == wanted
    pick = jnp.where(chosen, 1.0, 0.0).astype(BF16)
    mix = mix_ref[...]
    high = mix.astype(BF16)
    low = (mix - high.astype(F32)).astype(BF16)
    tiles = []
    for piece in (high, low):
        rows = lax.dot_general(
            pick, piece, (((1,), (0,)), ((), ())), preferred_element_type=F32
        ).astype(BF16)
        tiles.append(lax.dot_general(rows, pick, NT, preferred_element_type=F32).astype(BF16))
    tile = jnp.concatenate(tiles, axis=0)
    mixing_ref[...] = jnp.concatenate([tile, tile], axis=1)
    for source_ref, target_ref, scale in ((bias_ref, bias_out_ref, 1.0), (rate_ref, rate_out_ref, 0.5)):
        column = jnp.sum(jnp.where(chosen, source_ref[...], 0.0), axis=1, keepdims=True)
        target_ref[...] = jnp.broadcast_to(scale * column, target_ref.shape)


def exchanged(value):
    mine = value.shape[0] // (SIDE * SIDE)
    at = lambda a, b: (a * SIDE + b) * mine
    return jnp.concatenate(
        [value[at(b, a) : at(b, a) + mine] for a in range(SIDE) for b in range(SIDE)], axis=0
    )


def half_source(values, mixing, bias, rate):
    both = lax.dot_general(
        mixing, values, (((1,), (0,)), ((), ())), preferred_element_type=F32
    )
    half = both.shape[0] // 2
    inner = both[:half] + both[half:] + bias
    return rate * inner * jnp.exp(-0.125 * inner * inner)


def edges_kernel(
    total, side, origin_ref, place_ref, cols_ref, count_ref, low_ref, high_ref,
    mix_ref, bias_ref, rate_ref,
    to_right_ref, to_left_ref, mixing_ref, bias_out_ref, rate_out_ref,
):
    width, rows = cols_ref.shape
    for source_ref, target_ref, start in (
        (low_ref, to_right_ref, rows - REACH),
        (high_ref, to_left_ref, 0),
    ):
        for row in range(source_ref.shape[1]):
            n = start + row
            for d in range(width):
                wanted = origin_ref[0] * rows + n + d - REACH
                wanted = jnp.where(wanted < 0, wanted + total, wanted)
                wanted = jnp.where(wanted >= total, wanted - total, wanted)
                slot = jnp.int32(0)
                scale = jnp.float32(0.0)
                for r in range(width):
                    hit = jnp.logical_and(cols_ref[r, n] == wanted, r < count_ref[n])
                    slot = jnp.where(hit, r, slot)
                    scale = jnp.where(hit, 1.0, scale)
                for m in range(2):
                    target_ref[m, row, d] = source_ref[m, row, slot].astype(F32) * scale
    prepare_source(
        side, origin_ref[0], place_ref[0], mix_ref, bias_ref, rate_ref, mixing_ref, bias_out_ref, rate_out_ref
    )


def pack_edges(explicit_blocks, scalars, source, total, side):
    months, rows, width, block, _ = explicit_blocks.shape
    size = source[0].shape[0]
    spec = lambda count, at: pl.BlockSpec(
        (months, count, width, block, block), lambda i: (0, at, 0, 0, 0)
    )
    smem = pl.BlockSpec(memory_space=pltpu.SMEM)
    vmem = pl.BlockSpec(memory_space=pltpu.VMEM)
    shape = lambda count: jax.ShapeDtypeStruct((months, count, width, block, block), F32)
    return pl.pallas_call(
        functools.partial(edges_kernel, total, side),
        grid=(1,),
        in_specs=[smem] * 4
        + [spec(REACH, rows // REACH - 1), spec(REACH - 1, 0)]
        + [vmem] * 3,
        out_specs=[spec(REACH, 0), spec(REACH - 1, 0)] + [vmem] * 3,
        out_shape=[
            shape(REACH),
            shape(REACH - 1),
            jax.ShapeDtypeStruct((2 * size, 2 * size), BF16),
            jax.ShapeDtypeStruct((size, block), F32),
            jax.ShapeDtypeStruct((size, block), F32),
        ],
        compiler_params=pltpu.CompilerParams(vmem_limit_bytes=56 * MIB),
        name="edges",
    )(*scalars, explicit_blocks, explicit_blocks, *source)


def load_kernel(explicit_ref, implicit_ref, explicit_out_ref, implicit_out_ref, sems):
    chunks = sems.shape[1]
    copies = []
    for k, (source, target) in enumerate(
        ((explicit_ref, explicit_out_ref), (implicit_ref, implicit_out_ref))
    ):
        step = source.shape[1] // chunks
        for c in range(chunks):
            at = pl.ds(c * step, step)
            copies.append(
                pltpu.make_async_copy(source.at[:, at], target.at[:, at], sems.at[k, c])
            )
    for copy in copies:
        copy.start()
    for copy in copies:
        copy.wait()


def load(explicit_blocks, implicit_blocks):
    hbm = pl.BlockSpec(memory_space=pl.ANY)
    vmem = pl.BlockSpec(memory_space=pltpu.VMEM)
    return pl.pallas_call(
        load_kernel,
        in_specs=[hbm, hbm],
        out_specs=[vmem, vmem],
        out_shape=[
            pltpu.VMEM(explicit_blocks.shape, explicit_blocks.dtype),
            pltpu.VMEM(implicit_blocks.shape, implicit_blocks.dtype),
        ],
        scratch_shapes=[pltpu.SemaphoreType.DMA((2, 4))],
        compiler_params=pltpu.CompilerParams(vmem_limit_bytes=MIB),
        cost_estimate=pl.CostEstimate(flops=0, bytes_accessed=24 * MIB, transcendentals=0),
        name="load",
    )(explicit_blocks, implicit_blocks)


def first_kernel(
    total, origin_ref, cols_ref, count_ref, month_ref, weight_ref, explicit_ref, implicit_ref,
    near_ref, next_ref, far_ref, back_ref, left_ref, right_ref, mixing_ref, bias_ref, rate_ref,
    low_ref, high_ref, field_out_ref, values_ref, middle_ref,
):
    coef = coefficients(month_ref, weight_ref, 0)
    tables = (total, origin_ref, cols_ref, count_ref)
    rows = explicit_ref.shape[1]
    block = explicit_ref.shape[-1]
    tracers = bias_ref.shape[0]
    ext = rows + LOW + HIGH
    share = near_ref.shape[0] // ext
    zero = jnp.zeros((2 * tracers, block), BF16)
    values_ref[ext] = zero
    middle_ref[ext - REACH] = zero
    for b in range(ext):
        parts = [
            ref[pl.ds(b, share, stride=ext), :] for ref in (near_ref, next_ref, far_ref, back_ref)
        ]
        split_store(values_ref, b, jnp.concatenate(parts, axis=0))
    mixing, bias, rate = mixing_ref[...], bias_ref[...], rate_ref[...]

    def finish(frame, product):
        source = half_source(values_ref[frame + REACH], mixing, bias, rate)
        split_store(middle_ref, frame, product + source)

    for row in range(REACH):
        finish(row, edge_row(values_ref, left_ref, row, row, coef))
    for row in range(REACH - 1):
        frame = rows + REACH + row
        finish(frame, edge_row(values_ref, right_ref, row, frame, coef))
    for row in range(rows):
        finish(row + REACH, own_row(values_ref, explicit_ref, tables, row, 0, coef))

    for row in [*range(rows - LOW, rows), *range(rows - LOW)]:
        result = own_row(middle_ref, implicit_ref, tables, row, REACH, coef)
        split_store(field_out_ref, row, result)
        if row >= rows - LOW:
            at = row - (rows - LOW)
            low_ref[:, at * block : (at + 1) * block] = result
        if row < HIGH:
            high_ref[:, row * block : (row + 1) * block] = result


def inner_kernel(
    total, origin_ref, cols_ref, count_ref, month_ref, weight_ref, field_ref, explicit_ref, mixing_ref, bias_ref, rate_ref,
    middle_ref, values_ref,
):
    coef = coefficients(month_ref, weight_ref, 1)
    tables = (total, origin_ref, cols_ref, count_ref)
    rows = explicit_ref.shape[1]
    values_ref[LOW : LOW + rows] = field_ref[...]
    values_ref[rows + LOW + HIGH] = jnp.zeros(values_ref.shape[1:], BF16)
    mixing, bias, rate = mixing_ref[...], bias_ref[...], rate_ref[...]

    def explicit_row(row, carry):
        product = own_row(values_ref, explicit_ref, tables, row, 0, coef)
        source = half_source(values_ref[row + LOW], mixing, bias, rate)
        split_store(middle_ref, row, product + source)
        return carry

    for row in range(REACH, rows - REACH + 1):
        explicit_row(row, 0)


def last_kernel(
    total, origin_ref, cols_ref, count_ref, month_ref, weight_ref, low_in_ref, high_in_ref, field_ref, middle_in_ref,
    explicit_ref, implicit_ref, left_ref, right_ref, mixing_ref, bias_ref, rate_ref,
    out_ref, values_ref, middle_ref, result_ref,
):
    coef = coefficients(month_ref, weight_ref, 1)
    tables = (total, origin_ref, cols_ref, count_ref)
    rows = explicit_ref.shape[1]
    block = explicit_ref.shape[-1]
    tracers = bias_ref.shape[0]
    ext = rows + LOW + HIGH
    zero = jnp.zeros((2 * tracers, block), BF16)
    values_ref[ext] = zero
    middle_ref[ext - REACH] = zero
    values_ref[LOW : LOW + rows] = field_ref[...]
    middle_ref[2 * REACH : rows + 1] = middle_in_ref[REACH : rows - REACH + 1]
    for b in range(LOW):
        split_store(values_ref, b, exchanged(low_in_ref[:, b * block : (b + 1) * block]))
    for b in range(HIGH):
        value = exchanged(high_in_ref[:, b * block : (b + 1) * block])
        split_store(values_ref, LOW + rows + b, value)
    mixing, bias, rate = mixing_ref[...], bias_ref[...], rate_ref[...]

    def finish(frame, product):
        source = half_source(values_ref[frame + REACH], mixing, bias, rate)
        split_store(middle_ref, frame, product + source)

    for row in range(REACH):
        finish(row, edge_row(values_ref, left_ref, row, row, coef))
    for row in range(REACH - 1):
        frame = rows + REACH + row
        finish(frame, edge_row(values_ref, right_ref, row, frame, coef))
    for row in [*range(REACH), *range(rows - REACH + 1, rows)]:
        finish(row + REACH, own_row(values_ref, explicit_ref, tables, row, 0, coef))

    for row in range(rows):
        result_ref[:, row * block : (row + 1) * block] = own_row(
            middle_ref, implicit_ref, tables, row, REACH, coef
        )
    out_ref[...] = result_ref[: out_ref.shape[0], :]


def call(kernel, name, smem_count, hbm_count, args, outs, scratch, flops, limit):
    smem = pl.BlockSpec(memory_space=pltpu.SMEM)
    vmem = pl.BlockSpec(memory_space=pltpu.VMEM)
    hbm = pl.BlockSpec(memory_space=pltpu.HBM)
    return pl.pallas_call(
        kernel,
        in_specs=[smem] * smem_count
        + [hbm] * hbm_count
        + [vmem] * (len(args) - smem_count - hbm_count),
        out_specs=[vmem] * len(outs),
        out_shape=outs,
        scratch_shapes=scratch,
        compiler_params=pltpu.CompilerParams(vmem_limit_bytes=limit * MIB),
        cost_estimate=pl.CostEstimate(flops=flops, bytes_accessed=8 * MIB, transcendentals=0),
        name=name,
    )(*args)


def per_device(
    tracers,
    explicit_blocks,
    implicit_blocks,
    column_blocks,
    block_count,
    month_pair,
    weight_num,
    source_mix,
    source_bias,
    source_rate,
):
    rows, width = column_blocks.shape
    block = explicit_blocks.shape[-1]
    parts = lax.axis_size("pts")
    groups = lax.axis_size("trc")
    mine = tracers.shape[0]
    total = source_mix.shape[0]
    ext = rows + LOW + HIGH
    forward = [(i, (i + 1) % parts) for i in range(parts)]
    backward = [(target, source) for source, target in forward]

    low = lax.ppermute(tracers, "pts", forward)[:, -LOW * block :]
    high = lax.ppermute(tracers, "pts", backward)[:, : HIGH * block]
    origin = lax.axis_index("pts").astype(jnp.int32).reshape(1)
    place = lax.axis_index("trc").astype(jnp.int32).reshape(1)
    scalars = (origin, column_blocks.T, block_count, month_pair, weight_num)
    to_right, to_left, *source = pack_edges(
        explicit_blocks,
        (origin, place, column_blocks.T, block_count),
        (source_mix, source_bias[None], source_rate[None]),
        rows * parts,
        SIDE,
    )
    low, high, to_right, to_left = lax.optimization_barrier((low, high, to_right, to_left))
    extended = jnp.concatenate([low, tracers, high], axis=1).reshape(mine * ext, block)
    both = ("pts", "trc")

    def along(stage, k):
        moves = []
        for p in range(parts):
            for t in range(groups):
                y, x = divmod(t, SIDE)
                if (p + stage) % 2 == 0:
                    source_at = y * SIDE + (x + k) % SIDE
                else:
                    source_at = (y + k) % SIDE * SIDE + x
                moves.append((p * groups + source_at, p * groups + t))
        return moves

    line = jnp.concatenate(
        [extended] + [lax.ppermute(extended, both, along(0, k)) for k in range(1, SIDE)]
    )
    line, explicit_blocks, implicit_blocks = lax.optimization_barrier(
        (line, explicit_blocks, implicit_blocks)
    )
    gathered = [line] + [lax.ppermute(line, both, along(1, k)) for k in range(1, SIDE)]
    explicit_blocks, implicit_blocks = load(explicit_blocks, implicit_blocks)
    left = lax.ppermute(to_right, "pts", forward)
    right = lax.ppermute(to_left, "pts", backward)

    shape = jax.ShapeDtypeStruct
    stack = lambda count: pltpu.VMEM((count, 2 * total, block), BF16)
    one = 2 * 2 * total * 2 * block * width * block
    low, high, field = call(
        functools.partial(first_kernel, rows * parts), "first", 5, 0,
        (*scalars, explicit_blocks, implicit_blocks, *gathered, left, right, *source),
        [
            shape((total, LOW * block), F32),
            shape((total, HIGH * block), F32),
            shape((rows, 2 * total, block), BF16),
        ],
        [
            stack(ext + 1),
            stack(ext - REACH + 1),
        ],
        51 * one, 12,
    )
    low = lax.ppermute(low, "pts", forward)
    high = lax.ppermute(high, "pts", backward)
    (middle,) = call(
        functools.partial(inner_kernel, rows * parts), "inner", 5, 0,
        (*scalars, field, explicit_blocks, *source),
        [shape((rows, 2 * total, block), BF16)],
        [stack(ext + 1)],
        21 * one, 12,
    )
    (advanced,) = call(
        functools.partial(last_kernel, rows * parts), "last", 5, 0,
        (
            *scalars, low, high, field, middle, explicit_blocks, implicit_blocks,
            left, right, *source,
        ),
        [shape((mine, rows * block), F32)],
        [stack(ext + 1), stack(ext - REACH + 1), pltpu.VMEM((total, rows * block), F32)],
        30 * one, 12,
    )
    return advanced


def solution(mesh):
    in_specs = (
        P("trc", "pts"),
        P(None, "pts", None, None, None),
        P(None, "pts", None, None, None),
        P("pts", None),
        P("pts"),
        P(),
        P(),
        P(),
        P(),
        P(),
    )
    out_specs = P("trc", "pts")
    return jax.shard_map(
        per_device, mesh=mesh, in_specs=in_specs, out_specs=out_specs, check_vma=False
    )
```

```python
import functools

import jax
import jax.numpy as jnp
from jax import lax
from jax.experimental import pallas as pl
from jax.experimental.pallas import tpu as pltpu
from jax.sharding import PartitionSpec as P

REACH = 2
DAYS = 30
STEPS = 2
LOW = 2 * REACH
HIGH = 2 * (REACH - 1)
F32 = jnp.float32
BF16 = jnp.bfloat16
MIB = 1 << 20
SIDE = 4
NT = (((1,), (1,)), ((), ()))


def split_store(ref, where, value):
    half = value.shape[0]
    high = value.astype(BF16)
    ref[where, 0:half, :] = high
    ref[where, half : 2 * half, :] = (value - high.astype(F32)).astype(BF16)


def coefficients(month_ref, weight_ref, step):
    weight = weight_ref[step].astype(F32) * (1.0 / DAYS)
    straight = month_ref[0] == 0
    return (
        jnp.where(straight, 1.0 - weight, weight),
        jnp.where(straight, weight, 1.0 - weight),
    )


def combine(product, coef):
    block = product.shape[1] // 2
    half = product.shape[0] // 2
    mixed = coef[0] * product[:, :block] + coef[1] * product[:, block:]
    return mixed[:half] + mixed[half:]


def column(total, origin_ref, cols_ref, count_ref, row, r, spare):
    at = cols_ref[r, row] - origin_ref[0] * cols_ref.shape[1] + LOW
    at = jnp.where(at < 0, at + total, at)
    at = jnp.where(at >= total, at - total, at)
    return jnp.where(r < count_ref[row], at, spare)


def own_row(values_ref, blocks_ref, tables, row, shift, coef):
    width = blocks_ref.shape[2]
    spare = blocks_ref.shape[1] + LOW + HIGH
    left = jnp.concatenate(
        [values_ref[column(*tables, row, r, spare) - shift] for r in range(width)], axis=1
    )
    right = jnp.concatenate(
        [
            jnp.concatenate([blocks_ref[m, row, r] for r in range(width)], axis=1)
            for m in range(2)
        ],
        axis=0,
    )
    product = lax.dot_general(left, right, NT, preferred_element_type=F32)
    return combine(product, coef)


def edge_row(values_ref, edge_ref, row, first, coef):
    width = edge_ref.shape[2]
    left = jnp.concatenate([values_ref[first + d] for d in range(width)], axis=1)
    right = jnp.concatenate(
        [
            jnp.concatenate([edge_ref[m, row, d].astype(BF16) for d in range(width)], axis=1)
            for m in range(2)
        ],
        axis=0,
    )
    product = lax.dot_general(left, right, NT, preferred_element_type=F32)
    return combine(product, coef)


def prepare_source(side, part, place, mix_ref, bias_ref, rate_ref, mixing_ref, bias_out_ref, rate_out_ref):
    size = mix_ref.shape[0]
    mine = size // (side * side)
    at = lax.broadcasted_iota(jnp.int32, (size, size), 0)
    wanted = lax.broadcasted_iota(jnp.int32, (size, size), 1)
    outer, inner = at // (mine * side), lax.rem(at // mine, side)
    even = lax.rem(part, 2) == 0
    y = lax.rem(place // side + jnp.where(even, outer, inner), side)
    x = lax.rem(lax.rem(place, side) + jnp.where(even, inner, outer), side)
    chosen = (y * side + x) * mine + lax.rem(at, mine) == wanted
    pick = jnp.where(chosen, 1.0, 0.0).astype(BF16)
    mix = mix_ref[...]
    high = mix.astype(BF16)
    low = (mix - high.astype(F32)).astype(BF16)
    tiles = []
    for piece in (high, low):
        rows = lax.dot_general(
            pick, piece, (((1,), (0,)), ((), ())), preferred_element_type=F32
        ).astype(BF16)
        tiles.append(lax.dot_general(rows, pick, NT, preferred_element_type=F32).astype(BF16))
    tile = jnp.concatenate(tiles, axis=0)
    mixing_ref[...] = jnp.concatenate([tile, tile], axis=1)
    for source_ref, target_ref, scale in ((bias_ref, bias_out_ref, 1.0), (rate_ref, rate_out_ref, 0.5)):
        column = jnp.sum(jnp.where(chosen, source_ref[...], 0.0), axis=1, keepdims=True)
        target_ref[...] = jnp.broadcast_to(scale * column, target_ref.shape)


def exchanged(value):
    mine = value.shape[0] // (SIDE * SIDE)
    at = lambda a, b: (a * SIDE + b) * mine
    return jnp.concatenate(
        [value[at(b, a) : at(b, a) + mine] for a in range(SIDE) for b in range(SIDE)], axis=0
    )


def half_source(values, mixing, bias, rate):
    both = lax.dot_general(
        mixing, values, (((1,), (0,)), ((), ())), preferred_element_type=F32
    )
    half = both.shape[0] // 2
    inner = both[:half] + both[half:] + bias
    return rate * inner * jnp.exp(-0.125 * inner * inner)


def edges_kernel(
    total, side, origin_ref, place_ref, cols_ref, count_ref, low_ref, high_ref,
    mix_ref, bias_ref, rate_ref,
    to_right_ref, to_left_ref, mixing_ref, bias_out_ref, rate_out_ref,
):
    width, rows = cols_ref.shape
    for source_ref, target_ref, start in (
        (low_ref, to_right_ref, rows - REACH),
        (high_ref, to_left_ref, 0),
    ):
        for row in range(source_ref.shape[1]):
            n = start + row
            for d in range(width):
                wanted = origin_ref[0] * rows + n + d - REACH
                wanted = jnp.where(wanted < 0, wanted + total, wanted)
                wanted = jnp.where(wanted >= total, wanted - total, wanted)
                slot = jnp.int32(0)
                scale = jnp.float32(0.0)
                for r in range(width):
                    hit = jnp.logical_and(cols_ref[r, n] == wanted, r < count_ref[n])
                    slot = jnp.where(hit, r, slot)
                    scale = jnp.where(hit, 1.0, scale)
                for m in range(2):
                    target_ref[m, row, d] = source_ref[m, row, slot].astype(F32) * scale
    prepare_source(
        side, origin_ref[0], place_ref[0], mix_ref, bias_ref, rate_ref, mixing_ref, bias_out_ref, rate_out_ref
    )


def pack_edges(explicit_blocks, scalars, source, total, side):
    months, rows, width, block, _ = explicit_blocks.shape
    size = source[0].shape[0]
    spec = lambda count, at: pl.BlockSpec(
        (months, count, width, block, block), lambda i: (0, at, 0, 0, 0)
    )
    smem = pl.BlockSpec(memory_space=pltpu.SMEM)
    vmem = pl.BlockSpec(memory_space=pltpu.VMEM)
    shape = lambda count: jax.ShapeDtypeStruct((months, count, width, block, block), F32)
    return pl.pallas_call(
        functools.partial(edges_kernel, total, side),
        grid=(1,),
        in_specs=[smem] * 4
        + [spec(REACH, rows // REACH - 1), spec(REACH - 1, 0)]
        + [vmem] * 3,
        out_specs=[spec(REACH, 0), spec(REACH - 1, 0)] + [vmem] * 3,
        out_shape=[
            shape(REACH),
            shape(REACH - 1),
            jax.ShapeDtypeStruct((2 * size, 2 * size), BF16),
            jax.ShapeDtypeStruct((size, block), F32),
            jax.ShapeDtypeStruct((size, block), F32),
        ],
        compiler_params=pltpu.CompilerParams(vmem_limit_bytes=56 * MIB),
        name="edges",
    )(*scalars, explicit_blocks, explicit_blocks, *source)


def load_kernel(explicit_ref, implicit_ref, explicit_out_ref, implicit_out_ref, sems):
    chunks = sems.shape[1]
    copies = []
    for k, (source, target) in enumerate(
        ((explicit_ref, explicit_out_ref), (implicit_ref, implicit_out_ref))
    ):
        step = source.shape[1] // chunks
        for c in range(chunks):
            at = pl.ds(c * step, step)
            copies.append(
                pltpu.make_async_copy(source.at[:, at], target.at[:, at], sems.at[k, c])
            )
    for copy in copies:
        copy.start()
    for copy in copies:
        copy.wait()


def load(explicit_blocks, implicit_blocks):
    hbm = pl.BlockSpec(memory_space=pl.ANY)
    vmem = pl.BlockSpec(memory_space=pltpu.VMEM)
    return pl.pallas_call(
        load_kernel,
        in_specs=[hbm, hbm],
        out_specs=[vmem, vmem],
        out_shape=[
            pltpu.VMEM(explicit_blocks.shape, explicit_blocks.dtype),
            pltpu.VMEM(implicit_blocks.shape, implicit_blocks.dtype),
        ],
        scratch_shapes=[pltpu.SemaphoreType.DMA((2, 4))],
        compiler_params=pltpu.CompilerParams(vmem_limit_bytes=44 * MIB),
        cost_estimate=pl.CostEstimate(flops=0, bytes_accessed=24 * MIB, transcendentals=0),
        name="load",
    )(explicit_blocks, implicit_blocks)


def first_kernel(
    total, origin_ref, cols_ref, count_ref, month_ref, weight_ref, explicit_ref, implicit_ref,
    near_ref, next_ref, far_ref, back_ref, left_ref, right_ref, mixing_ref, bias_ref, rate_ref,
    low_ref, high_ref, field_out_ref, values_ref, middle_ref,
):
    coef = coefficients(month_ref, weight_ref, 0)
    tables = (total, origin_ref, cols_ref, count_ref)
    rows = explicit_ref.shape[1]
    block = explicit_ref.shape[-1]
    tracers = bias_ref.shape[0]
    ext = rows + LOW + HIGH
    share = near_ref.shape[0] // ext
    zero = jnp.zeros((2 * tracers, block), BF16)
    values_ref[ext] = zero
    middle_ref[ext - REACH] = zero
    for b in range(ext):
        parts = [
            ref[pl.ds(b, share, stride=ext), :] for ref in (near_ref, next_ref, far_ref, back_ref)
        ]
        split_store(values_ref, b, jnp.concatenate(parts, axis=0))
    mixing, bias, rate = mixing_ref[...], bias_ref[...], rate_ref[...]

    def finish(frame, product):
        source = half_source(values_ref[frame + REACH], mixing, bias, rate)
        split_store(middle_ref, frame, product + source)

    for row in range(REACH):
        finish(row, edge_row(values_ref, left_ref, row, row, coef))
    for row in range(REACH - 1):
        frame = rows + REACH + row
        finish(frame, edge_row(values_ref, right_ref, row, frame, coef))
    for row in range(rows):
        finish(row + REACH, own_row(values_ref, explicit_ref, tables, row, 0, coef))

    for row in [*range(rows - LOW, rows), *range(rows - LOW)]:
        result = own_row(middle_ref, implicit_ref, tables, row, REACH, coef)
        split_store(field_out_ref, row, result)
        if row >= rows - LOW:
            at = row - (rows - LOW)
            low_ref[:, at * block : (at + 1) * block] = result
        if row < HIGH:
            high_ref[:, row * block : (row + 1) * block] = result


def inner_kernel(
    total, origin_ref, cols_ref, count_ref, month_ref, weight_ref, field_ref, explicit_ref, mixing_ref, bias_ref, rate_ref,
    middle_ref, values_ref,
):
    coef = coefficients(month_ref, weight_ref, 1)
    tables = (total, origin_ref, cols_ref, count_ref)
    rows = explicit_ref.shape[1]
    values_ref[LOW : LOW + rows] = field_ref[...]
    values_ref[rows + LOW + HIGH] = jnp.zeros(values_ref.shape[1:], BF16)
    mixing, bias, rate = mixing_ref[...], bias_ref[...], rate_ref[...]

    def explicit_row(row, carry):
        product = own_row(values_ref, explicit_ref, tables, row, 0, coef)
        source = half_source(values_ref[row + LOW], mixing, bias, rate)
        split_store(middle_ref, row, product + source)
        return carry

    for row in range(REACH, rows - REACH + 1):
        explicit_row(row, 0)


def last_kernel(
    total, origin_ref, cols_ref, count_ref, month_ref, weight_ref, low_in_ref, high_in_ref, field_ref, middle_in_ref,
    explicit_ref, implicit_ref, left_ref, right_ref, mixing_ref, bias_ref, rate_ref,
    out_ref, values_ref, middle_ref, result_ref,
):
    coef = coefficients(month_ref, weight_ref, 1)
    tables = (total, origin_ref, cols_ref, count_ref)
    rows = explicit_ref.shape[1]
    block = explicit_ref.shape[-1]
    tracers = bias_ref.shape[0]
    ext = rows + LOW + HIGH
    zero = jnp.zeros((2 * tracers, block), BF16)
    values_ref[ext] = zero
    middle_ref[ext - REACH] = zero
    values_ref[LOW : LOW + rows] = field_ref[...]
    middle_ref[2 * REACH : rows + 1] = middle_in_ref[REACH : rows - REACH + 1]
    for b in range(LOW):
        split_store(values_ref, b, exchanged(low_in_ref[:, b * block : (b + 1) * block]))
    for b in range(HIGH):
        value = exchanged(high_in_ref[:, b * block : (b + 1) * block])
        split_store(values_ref, LOW + rows + b, value)
    mixing, bias, rate = mixing_ref[...], bias_ref[...], rate_ref[...]

    def finish(frame, product):
        source = half_source(values_ref[frame + REACH], mixing, bias, rate)
        split_store(middle_ref, frame, product + source)

    for row in range(REACH):
        finish(row, edge_row(values_ref, left_ref, row, row, coef))
    for row in range(REACH - 1):
        frame = rows + REACH + row
        finish(frame, edge_row(values_ref, right_ref, row, frame, coef))
    for row in [*range(REACH), *range(rows - REACH + 1, rows)]:
        finish(row + REACH, own_row(values_ref, explicit_ref, tables, row, 0, coef))

    for row in range(rows):
        result_ref[:, row * block : (row + 1) * block] = own_row(
            middle_ref, implicit_ref, tables, row, REACH, coef
        )
    out_ref[...] = result_ref[: out_ref.shape[0], :]


def call(kernel, name, smem_count, hbm_count, args, outs, scratch, flops, limit):
    smem = pl.BlockSpec(memory_space=pltpu.SMEM)
    vmem = pl.BlockSpec(memory_space=pltpu.VMEM)
    hbm = pl.BlockSpec(memory_space=pltpu.HBM)
    return pl.pallas_call(
        kernel,
        in_specs=[smem] * smem_count
        + [hbm] * hbm_count
        + [vmem] * (len(args) - smem_count - hbm_count),
        out_specs=[vmem] * len(outs),
        out_shape=outs,
        scratch_shapes=scratch,
        compiler_params=pltpu.CompilerParams(vmem_limit_bytes=limit * MIB),
        cost_estimate=pl.CostEstimate(flops=flops, bytes_accessed=8 * MIB, transcendentals=0),
        name=name,
    )(*args)


def per_device(
    tracers,
    explicit_blocks,
    implicit_blocks,
    column_blocks,
    block_count,
    month_pair,
    weight_num,
    source_mix,
    source_bias,
    source_rate,
):
    rows, width = column_blocks.shape
    block = explicit_blocks.shape[-1]
    parts = lax.axis_size("pts")
    groups = lax.axis_size("trc")
    mine = tracers.shape[0]
    total = source_mix.shape[0]
    ext = rows + LOW + HIGH
    forward = [(i, (i + 1) % parts) for i in range(parts)]
    backward = [(target, source) for source, target in forward]

    low = lax.ppermute(tracers, "pts", forward)[:, -LOW * block :]
    high = lax.ppermute(tracers, "pts", backward)[:, : HIGH * block]
    origin = lax.axis_index("pts").astype(jnp.int32).reshape(1)
    place = lax.axis_index("trc").astype(jnp.int32).reshape(1)
    scalars = (origin, column_blocks.T, block_count, month_pair, weight_num)
    to_right, to_left, *source = pack_edges(
        explicit_blocks,
        (origin, place, column_blocks.T, block_count),
        (source_mix, source_bias[None], source_rate[None]),
        rows * parts,
        SIDE,
    )
    low, high, to_right, to_left = lax.optimization_barrier((low, high, to_right, to_left))
    extended = jnp.concatenate([low, tracers, high], axis=1).reshape(mine * ext, block)
    both = ("pts", "trc")

    def along(stage, k):
        moves = []
        for p in range(parts):
            for t in range(groups):
                y, x = divmod(t, SIDE)
                if (p + stage) % 2 == 0:
                    source_at = y * SIDE + (x + k) % SIDE
                else:
                    source_at = (y + k) % SIDE * SIDE + x
                moves.append((p * groups + source_at, p * groups + t))
        return moves

    line = jnp.concatenate(
        [extended] + [lax.ppermute(extended, both, along(0, k)) for k in range(1, SIDE)]
    )
    line, explicit_blocks, implicit_blocks = lax.optimization_barrier(
        (line, explicit_blocks, implicit_blocks)
    )
    gathered = [line] + [lax.ppermute(line, both, along(1, k)) for k in range(1, SIDE)]
    explicit_blocks, implicit_blocks = load(explicit_blocks, implicit_blocks)
    left = lax.ppermute(to_right, "pts", forward)
    right = lax.ppermute(to_left, "pts", backward)

    shape = jax.ShapeDtypeStruct
    stack = lambda count: pltpu.VMEM((count, 2 * total, block), BF16)
    one = 2 * 2 * total * 2 * block * width * block
    low, high, field = call(
        functools.partial(first_kernel, rows * parts), "first", 5, 0,
        (*scalars, explicit_blocks, implicit_blocks, *gathered, left, right, *source),
        [
            shape((total, LOW * block), F32),
            shape((total, HIGH * block), F32),
            shape((rows, 2 * total, block), BF16),
        ],
        [
            stack(ext + 1),
            stack(ext - REACH + 1),
        ],
        51 * one, 12,
    )
    low = lax.ppermute(low, "pts", forward)
    high = lax.ppermute(high, "pts", backward)
    (middle,) = call(
        functools.partial(inner_kernel, rows * parts), "inner", 5, 0,
        (*scalars, field, explicit_blocks, *source),
        [shape((rows, 2 * total, block), BF16)],
        [stack(ext + 1)],
        21 * one, 12,
    )
    (advanced,) = call(
        functools.partial(last_kernel, rows * parts), "last", 5, 0,
        (
            *scalars, low, high, field, middle, explicit_blocks, implicit_blocks,
            left, right, *source,
        ),
        [shape((mine, rows * block), F32)],
        [stack(ext + 1), stack(ext - REACH + 1), pltpu.VMEM((total, rows * block), F32)],
        30 * one, 12,
    )
    return advanced


def solution(mesh):
    in_specs = (
        P("trc", "pts"),
        P(None, "pts", None, None, None),
        P(None, "pts", None, None, None),
        P("pts", None),
        P("pts"),
        P(),
        P(),
        P(),
        P(),
        P(),
    )
    out_specs = P("trc", "pts")
    return jax.shard_map(
        per_device, mesh=mesh, in_specs=in_specs, out_specs=out_specs, check_vma=False
    )
```

```python
import functools

import jax
import jax.numpy as jnp
from jax import lax
from jax.experimental import pallas as pl
from jax.experimental.pallas import tpu as pltpu
from jax.sharding import PartitionSpec as P

REACH = 2
DAYS = 30
STEPS = 2
LOW = 2 * REACH
HIGH = 2 * (REACH - 1)
F32 = jnp.float32
BF16 = jnp.bfloat16
MIB = 1 << 20
SIDE = 4
TILE = 16
NT = (((1,), (1,)), ((), ()))


def split_store(ref, where, value):
    half = value.shape[0]
    high = value.astype(BF16)
    ref[where, 0:half, :] = high
    ref[where, half : 2 * half, :] = (value - high.astype(F32)).astype(BF16)


def coefficients(month_ref, weight_ref, step):
    weight = weight_ref[step].astype(F32) * (1.0 / DAYS)
    straight = month_ref[0] == 0
    return (
        jnp.where(straight, 1.0 - weight, weight),
        jnp.where(straight, weight, 1.0 - weight),
    )


def own_store(ref, where, value):
    high = value.astype(BF16).astype(F32)
    spare = jnp.zeros((TILE - 2 * value.shape[0], value.shape[1]), F32)
    ref[where] = jnp.concatenate([high, value - high, spare], axis=0).astype(BF16)


def combine(product, coef, half):
    block = product.shape[1] // 2
    mixed = coef[0] * product[:, :block] + coef[1] * product[:, block:]
    return mixed[:half] + mixed[half : 2 * half]


def column(total, origin_ref, cols_ref, count_ref, row, r, spare):
    at = cols_ref[r, row] - origin_ref[0] * cols_ref.shape[1] + LOW
    at = jnp.where(at < 0, at + total, at)
    at = jnp.where(at >= total, at - total, at)
    return jnp.where(r < count_ref[row], at, spare)


def own_row(values_ref, blocks_ref, tables, row, shift, coef, half):
    width = blocks_ref.shape[2]
    spare = blocks_ref.shape[1] + LOW + HIGH
    left = jnp.concatenate(
        [values_ref[column(*tables, row, r, spare) - shift] for r in range(width)], axis=1
    )
    right = jnp.concatenate(
        [
            jnp.concatenate([blocks_ref[m, row, r] for r in range(width)], axis=1)
            for m in range(2)
        ],
        axis=0,
    )
    product = lax.dot_general(left, right, NT, preferred_element_type=F32)
    return combine(product, coef, half)


def edge_row(values_ref, edge_ref, row, first, coef, half):
    width = edge_ref.shape[2]
    left = jnp.concatenate([values_ref[first + d] for d in range(width)], axis=1)
    right = jnp.concatenate(
        [
            jnp.concatenate([edge_ref[m, row, d].astype(BF16) for d in range(width)], axis=1)
            for m in range(2)
        ],
        axis=0,
    )
    product = lax.dot_general(left, right, NT, preferred_element_type=F32)
    return combine(product, coef, half)


def prepare_source(side, part, place, mix_ref, bias_ref, rate_ref, mixing_ref, own_ref, bias_out_ref, rate_out_ref):
    size = mix_ref.shape[0]
    mine = size // (side * side)
    at = lax.broadcasted_iota(jnp.int32, (size, size), 0)
    wanted = lax.broadcasted_iota(jnp.int32, (size, size), 1)
    outer, inner = at // (mine * side), lax.rem(at // mine, side)
    even = lax.rem(part, 2) == 0
    y = lax.rem(place // side + side - jnp.where(even, outer, inner), side)
    x = lax.rem(lax.rem(place, side) + side - jnp.where(even, inner, outer), side)
    chosen = (y * side + x) * mine + lax.rem(at, mine) == wanted
    pick = jnp.where(chosen, 1.0, 0.0).astype(BF16)
    mix = mix_ref[...]
    high = mix.astype(BF16)
    low = (mix - high.astype(F32)).astype(BF16)
    tiles = []
    for piece in (high, low):
        rows = lax.dot_general(
            pick, piece, (((1,), (0,)), ((), ())), preferred_element_type=F32
        ).astype(BF16)
        tiles.append(lax.dot_general(rows, pick, NT, preferred_element_type=F32))
    tile = jnp.concatenate(tiles, axis=0).astype(BF16)
    mixing_ref[...] = jnp.concatenate([tile, tile], axis=1)
    spare = jnp.zeros((TILE - 2 * mine, size), F32)
    tile = jnp.concatenate([tiles[0][:mine], tiles[1][:mine], spare], axis=0).astype(BF16)
    own_ref[...] = jnp.concatenate([tile, tile], axis=1)
    for source_ref, target_ref, scale in ((bias_ref, bias_out_ref, 1.0), (rate_ref, rate_out_ref, 0.5)):
        column = jnp.sum(jnp.where(chosen, source_ref[...], 0.0), axis=1, keepdims=True)
        target_ref[...] = jnp.broadcast_to(scale * column, target_ref.shape)


def exchanged(value):
    mine = value.shape[0] // (SIDE * SIDE)
    at = lambda a, b: (a * SIDE + b) * mine
    return jnp.concatenate(
        [value[at(b, a) : at(b, a) + mine] for a in range(SIDE) for b in range(SIDE)], axis=0
    )


def half_source(values, mixing, bias, rate):
    both = lax.dot_general(
        mixing, values, (((1,), (0,)), ((), ())), preferred_element_type=F32
    )
    half = bias.shape[0]
    inner = both[:half] + both[half : 2 * half] + bias
    return rate * inner * jnp.exp(-0.125 * inner * inner)


def edges_kernel(
    total, side, origin_ref, place_ref, cols_ref, count_ref, low_ref, high_ref,
    mix_ref, bias_ref, rate_ref,
    to_right_ref, to_left_ref, mixing_ref, own_ref, bias_out_ref, rate_out_ref,
):
    width, rows = cols_ref.shape
    for source_ref, target_ref, start in (
        (low_ref, to_right_ref, rows - REACH),
        (high_ref, to_left_ref, 0),
    ):
        for row in range(source_ref.shape[1]):
            n = start + row
            for d in range(width):
                wanted = origin_ref[0] * rows + n + d - REACH
                wanted = jnp.where(wanted < 0, wanted + total, wanted)
                wanted = jnp.where(wanted >= total, wanted - total, wanted)
                slot = jnp.int32(0)
                scale = jnp.float32(0.0)
                for r in range(width):
                    hit = jnp.logical_and(cols_ref[r, n] == wanted, r < count_ref[n])
                    slot = jnp.where(hit, r, slot)
                    scale = jnp.where(hit, 1.0, scale)
                for m in range(2):
                    target_ref[m, row, d] = source_ref[m, row, slot].astype(F32) * scale
    prepare_source(
        side, origin_ref[0], place_ref[0], mix_ref, bias_ref, rate_ref,
        mixing_ref, own_ref, bias_out_ref, rate_out_ref,
    )


def pack_edges(explicit_blocks, scalars, source, total, side):
    months, rows, width, block, _ = explicit_blocks.shape
    size = source[0].shape[0]
    spec = lambda count, at: pl.BlockSpec(
        (months, count, width, block, block), lambda i: (0, at, 0, 0, 0)
    )
    smem = pl.BlockSpec(memory_space=pltpu.SMEM)
    vmem = pl.BlockSpec(memory_space=pltpu.VMEM)
    shape = lambda count: jax.ShapeDtypeStruct((months, count, width, block, block), F32)
    return pl.pallas_call(
        functools.partial(edges_kernel, total, side),
        grid=(1,),
        in_specs=[smem] * 4
        + [spec(REACH, rows // REACH - 1), spec(REACH - 1, 0)]
        + [vmem] * 3,
        out_specs=[spec(REACH, 0), spec(REACH - 1, 0)] + [vmem] * 4,
        out_shape=[
            shape(REACH),
            shape(REACH - 1),
            jax.ShapeDtypeStruct((2 * size, 2 * size), BF16),
            jax.ShapeDtypeStruct((TILE, 2 * size), BF16),
            jax.ShapeDtypeStruct((size, block), F32),
            jax.ShapeDtypeStruct((size, block), F32),
        ],
        compiler_params=pltpu.CompilerParams(vmem_limit_bytes=56 * MIB),
        name="edges",
    )(*scalars, explicit_blocks, explicit_blocks, *source)


def load_kernel(explicit_ref, implicit_ref, explicit_out_ref, implicit_out_ref, sems):
    chunks = sems.shape[1]
    copies = []
    for k, (source, target) in enumerate(
        ((explicit_ref, explicit_out_ref), (implicit_ref, implicit_out_ref))
    ):
        step = source.shape[1] // chunks
        for c in range(chunks):
            at = pl.ds(c * step, step)
            copies.append(
                pltpu.make_async_copy(source.at[:, at], target.at[:, at], sems.at[k, c])
            )
    for copy in copies:
        copy.start()
    for copy in copies:
        copy.wait()


def load(explicit_blocks, implicit_blocks):
    hbm = pl.BlockSpec(memory_space=pl.ANY)
    vmem = pl.BlockSpec(memory_space=pltpu.VMEM)
    return pl.pallas_call(
        load_kernel,
        in_specs=[hbm, hbm],
        out_specs=[vmem, vmem],
        out_shape=[
            pltpu.VMEM(explicit_blocks.shape, explicit_blocks.dtype),
            pltpu.VMEM(implicit_blocks.shape, implicit_blocks.dtype),
        ],
        scratch_shapes=[pltpu.SemaphoreType.DMA((2, 4))],
        compiler_params=pltpu.CompilerParams(vmem_limit_bytes=44 * MIB),
        cost_estimate=pl.CostEstimate(flops=0, bytes_accessed=24 * MIB, transcendentals=0),
        name="load",
    )(explicit_blocks, implicit_blocks)


def first_kernel(
    total, origin_ref, cols_ref, count_ref, month_ref, weight_ref, explicit_ref, implicit_ref,
    near_ref, next_ref, far_ref, back_ref, left_ref, right_ref, mixing_ref, bias_ref, rate_ref,
    low_ref, high_ref, middle_ref, values_ref,
):
    coef = coefficients(month_ref, weight_ref, 0)
    tables = (total, origin_ref, cols_ref, count_ref)
    rows = explicit_ref.shape[1]
    block = explicit_ref.shape[-1]
    tracers = bias_ref.shape[0]
    ext = rows + LOW + HIGH
    share = near_ref.shape[0] // ext
    zero = jnp.zeros((2 * tracers, block), BF16)
    values_ref[ext] = zero
    middle_ref[ext - REACH] = zero
    for b in range(ext):
        parts = [
            ref[pl.ds(b, share, stride=ext), :] for ref in (near_ref, next_ref, far_ref, back_ref)
        ]
        split_store(values_ref, b, jnp.concatenate(parts, axis=0))
    mixing, bias, rate = mixing_ref[...], bias_ref[...], rate_ref[...]

    def finish(frame, product):
        source = half_source(values_ref[frame + REACH], mixing, bias, rate)
        split_store(middle_ref, frame, product + source)

    for row in range(REACH):
        finish(row, edge_row(values_ref, left_ref, row, row, coef, tracers))
    for row in range(REACH - 1):
        frame = rows + REACH + row
        finish(frame, edge_row(values_ref, right_ref, row, frame, coef, tracers))
    for row in range(rows):
        finish(row + REACH, own_row(values_ref, explicit_ref, tables, row, 0, coef, tracers))
    for at in range(LOW):
        low_ref[:, at * block : (at + 1) * block] = own_row(
            middle_ref, implicit_ref, tables, rows - LOW + at, REACH, coef, tracers
        )
    for row in range(HIGH):
        high_ref[:, row * block : (row + 1) * block] = own_row(
            middle_ref, implicit_ref, tables, row, REACH, coef, tracers
        )


def inner_kernel(
    total, origin_ref, cols_ref, count_ref, month_ref, weight_ref, explicit_ref, implicit_ref,
    low_ref, high_ref, middle_ref, mixing_ref, bias_ref, rate_ref,
    field_ref, own_ref, own_middle_ref,
):
    coef = coefficients(month_ref, weight_ref, 0)
    tables = (total, origin_ref, cols_ref, count_ref)
    rows = explicit_ref.shape[1]
    block = explicit_ref.shape[-1]
    tracers = low_ref.shape[0]
    mine = bias_ref.shape[0] // (SIDE * SIDE)
    ext = rows + LOW + HIGH

    def put(row, result):
        split_store(field_ref, row, result)
        own_store(own_ref, row + LOW, result[:mine])

    for at in range(LOW):
        put(rows - LOW + at, low_ref[:, at * block : (at + 1) * block])
    for row in range(HIGH):
        put(row, high_ref[:, row * block : (row + 1) * block])
    for row in range(HIGH, rows - LOW):
        put(row, own_row(middle_ref, implicit_ref, tables, row, REACH, coef, tracers))
    own_ref[ext] = jnp.zeros((TILE, block), BF16)
    coef = coefficients(month_ref, weight_ref, 1)
    mixing, bias, rate = mixing_ref[...], bias_ref[:mine, :], rate_ref[:mine, :]
    for row in range(REACH, rows - REACH + 1):
        product = own_row(own_ref, explicit_ref, tables, row, 0, coef, mine)
        source = half_source(field_ref[row], mixing, bias, rate)
        own_store(own_middle_ref, row + REACH, product + source)


def last_kernel(
    total, origin_ref, cols_ref, count_ref, month_ref, weight_ref, low_in_ref, high_in_ref,
    field_ref, own_in_ref, own_middle_in_ref, explicit_ref, implicit_ref, left_ref, right_ref,
    mixing_ref, bias_ref, rate_ref, out_ref, halo_ref, own_ref, own_middle_ref,
):
    coef = coefficients(month_ref, weight_ref, 1)
    tables = (total, origin_ref, cols_ref, count_ref)
    rows = explicit_ref.shape[1]
    block = explicit_ref.shape[-1]
    mine = bias_ref.shape[0] // (SIDE * SIDE)
    ext = rows + LOW + HIGH
    own_ref[LOW : LOW + rows] = own_in_ref[LOW : LOW + rows]
    own_ref[ext] = jnp.zeros((TILE, block), BF16)
    own_middle_ref[2 * REACH : rows + 1] = own_middle_in_ref[2 * REACH : rows + 1]
    own_middle_ref[ext - REACH] = jnp.zeros((TILE, block), BF16)
    for b in range(LOW + HIGH):
        if b < LOW:
            value, frame = low_in_ref[:, b * block : (b + 1) * block], b
        else:
            value, frame = high_in_ref[:, (b - LOW) * block : (b - LOW + 1) * block], rows + b
        value = exchanged(value)
        split_store(halo_ref, b, value)
        own_store(own_ref, frame, value[:mine])
    mixing, bias, rate = mixing_ref[...], bias_ref[:mine, :], rate_ref[:mine, :]

    def finish(frame, values, product):
        own_store(own_middle_ref, frame, product + half_source(values, mixing, bias, rate))

    for row in range(REACH):
        product = edge_row(own_ref, left_ref, row, row, coef, mine)
        finish(row, halo_ref[row + REACH], product)
    for row in range(REACH - 1):
        frame = rows + REACH + row
        product = edge_row(own_ref, right_ref, row, frame, coef, mine)
        finish(frame, halo_ref[LOW + row], product)
    for row in [*range(REACH), *range(rows - REACH + 1, rows)]:
        product = own_row(own_ref, explicit_ref, tables, row, 0, coef, mine)
        finish(row + REACH, field_ref[row], product)
    for row in range(rows):
        out_ref[:, row * block : (row + 1) * block] = own_row(
            own_middle_ref, implicit_ref, tables, row, REACH, coef, mine
        )


def call(kernel, name, smem_count, hbm_count, args, outs, scratch, flops, limit):
    smem = pl.BlockSpec(memory_space=pltpu.SMEM)
    vmem = pl.BlockSpec(memory_space=pltpu.VMEM)
    hbm = pl.BlockSpec(memory_space=pltpu.HBM)
    return pl.pallas_call(
        kernel,
        in_specs=[smem] * smem_count
        + [hbm] * hbm_count
        + [vmem] * (len(args) - smem_count - hbm_count),
        out_specs=[vmem] * len(outs),
        out_shape=outs,
        scratch_shapes=scratch,
        compiler_params=pltpu.CompilerParams(vmem_limit_bytes=limit * MIB),
        cost_estimate=pl.CostEstimate(flops=flops, bytes_accessed=8 * MIB, transcendentals=0),
        name=name,
    )(*args)


def per_device(
    tracers,
    explicit_blocks,
    implicit_blocks,
    column_blocks,
    block_count,
    month_pair,
    weight_num,
    source_mix,
    source_bias,
    source_rate,
):
    rows, width = column_blocks.shape
    block = explicit_blocks.shape[-1]
    parts = lax.axis_size("pts")
    groups = lax.axis_size("trc")
    mine = tracers.shape[0]
    total = source_mix.shape[0]
    ext = rows + LOW + HIGH
    forward = [(i, (i + 1) % parts) for i in range(parts)]
    backward = [(target, source) for source, target in forward]

    low = lax.ppermute(tracers, "pts", forward)[:, -LOW * block :]
    high = lax.ppermute(tracers, "pts", backward)[:, : HIGH * block]
    origin = lax.axis_index("pts").astype(jnp.int32).reshape(1)
    place = lax.axis_index("trc").astype(jnp.int32).reshape(1)
    scalars = (origin, column_blocks.T, block_count, month_pair, weight_num)
    to_right, to_left, *source = pack_edges(
        explicit_blocks,
        (origin, place, column_blocks.T, block_count),
        (source_mix, source_bias[None], source_rate[None]),
        rows * parts,
        SIDE,
    )
    low, high, to_right, to_left = lax.optimization_barrier((low, high, to_right, to_left))
    extended = jnp.concatenate([low, tracers, high], axis=1).reshape(mine * ext, block)
    both = ("pts", "trc")

    def along(stage, k):
        moves = []
        for p in range(parts):
            for t in range(groups):
                y, x = divmod(t, SIDE)
                if (p + stage) % 2 == 0:
                    source_at = y * SIDE + (x - k) % SIDE
                else:
                    source_at = (y - k) % SIDE * SIDE + x
                moves.append((p * groups + source_at, p * groups + t))
        return moves

    line = jnp.concatenate(
        [extended] + [lax.ppermute(extended, both, along(0, k)) for k in range(1, SIDE)]
    )
    line, explicit_blocks, implicit_blocks = lax.optimization_barrier(
        (line, explicit_blocks, implicit_blocks)
    )
    gathered = [line] + [lax.ppermute(line, both, along(1, k)) for k in range(1, SIDE)]
    explicit_blocks, implicit_blocks = load(explicit_blocks, implicit_blocks)
    left = lax.ppermute(to_right, "pts", forward)
    right = lax.ppermute(to_left, "pts", backward)

    shape = jax.ShapeDtypeStruct
    stack = lambda count: pltpu.VMEM((count, 2 * total, block), BF16)
    one = 2 * 2 * total * 2 * block * width * block
    own = lambda count: shape((count, TILE, block), BF16)
    mixing, own_mixing, bias, rate = source
    own_source = (own_mixing, bias, rate)
    low, high, middle = call(
        functools.partial(first_kernel, rows * parts), "first", 5, 0,
        (
            *scalars, explicit_blocks, implicit_blocks, *gathered, left, right,
            mixing, bias, rate,
        ),
        [
            shape((total, LOW * block), F32),
            shape((total, HIGH * block), F32),
            shape((ext - REACH + 1, 2 * total, block), BF16),
        ],
        [stack(ext + 1)],
        33 * one, 12,
    )
    low_in = lax.ppermute(low, "pts", forward)
    high_in = lax.ppermute(high, "pts", backward)
    field, own_field, own_middle = call(
        functools.partial(inner_kernel, rows * parts), "inner", 5, 0,
        (*scalars, explicit_blocks, implicit_blocks, low, high, middle, *own_source),
        [shape((rows, 2 * total, block), BF16), own(ext + 1), own(ext - REACH + 1)],
        [],
        39 * one, 12,
    )
    (advanced,) = call(
        functools.partial(last_kernel, rows * parts), "last", 5, 0,
        (
            *scalars, low_in, high_in, field, own_field, own_middle,
            explicit_blocks, implicit_blocks, left, right, *own_source,
        ),
        [shape((mine, rows * block), F32)],
        [
            stack(LOW + HIGH),
            pltpu.VMEM((ext + 1, TILE, block), BF16),
            pltpu.VMEM((ext - REACH + 1, TILE, block), BF16),
        ],
        30 * one, 12,
    )
    return advanced


def solution(mesh):
    in_specs = (
        P("trc", "pts"),
        P(None, "pts", None, None, None),
        P(None, "pts", None, None, None),
        P("pts", None),
        P("pts"),
        P(),
        P(),
        P(),
        P(),
        P(),
    )
    out_specs = P("trc", "pts")
    return jax.shard_map(
        per_device, mesh=mesh, in_specs=in_specs, out_specs=out_specs, check_vma=False
    )
```

```python
import functools

import jax
import jax.numpy as jnp
from jax import lax
from jax.experimental import pallas as pl
from jax.experimental.pallas import tpu as pltpu
from jax.sharding import PartitionSpec as P

REACH = 2
DAYS = 30
STEPS = 2
LOW = 2 * REACH
HIGH = 2 * (REACH - 1)
F32 = jnp.float32
BF16 = jnp.bfloat16
MIB = 1 << 20
SIDE = 4
TILE = 16
NT = (((1,), (1,)), ((), ()))


def split_store(ref, where, value):
    half = value.shape[0]
    high = value.astype(BF16)
    ref[where, 0:half, :] = high
    ref[where, half : 2 * half, :] = (value - high.astype(F32)).astype(BF16)


def coefficients(month_ref, weight_ref, step):
    weight = weight_ref[step].astype(F32) * (1.0 / DAYS)
    straight = month_ref[0] == 0
    return (
        jnp.where(straight, 1.0 - weight, weight),
        jnp.where(straight, weight, 1.0 - weight),
    )


def own_store(ref, where, value):
    high = value.astype(BF16).astype(F32)
    spare = jnp.zeros((TILE - 2 * value.shape[0], value.shape[1]), F32)
    ref[where] = jnp.concatenate([high, value - high, spare], axis=0).astype(BF16)


def combine(product, coef, half):
    block = product.shape[1] // 2
    mixed = coef[0] * product[:, :block] + coef[1] * product[:, block:]
    return mixed[:half] + mixed[half : 2 * half]


def column(total, origin_ref, cols_ref, count_ref, row, r, spare):
    at = cols_ref[r, row] - origin_ref[0] * cols_ref.shape[1] + LOW
    at = jnp.where(at < 0, at + total, at)
    at = jnp.where(at >= total, at - total, at)
    return jnp.where(r < count_ref[row], at, spare)


def own_row(values_ref, blocks_ref, tables, row, shift, coef, half):
    width = blocks_ref.shape[2]
    spare = blocks_ref.shape[1] + LOW + HIGH
    left = jnp.concatenate(
        [values_ref[column(*tables, row, r, spare) - shift] for r in range(width)], axis=1
    )
    right = jnp.concatenate(
        [
            jnp.concatenate([blocks_ref[m, row, r] for r in range(width)], axis=1)
            for m in range(2)
        ],
        axis=0,
    )
    product = lax.dot_general(left, right, NT, preferred_element_type=F32)
    return combine(product, coef, half)


def tile_row(values_ref, tiles_ref, tables, row, coef, half):
    width = tables[2].shape[0]
    spare = tiles_ref.shape[0] + LOW + HIGH
    left = jnp.concatenate(
        [values_ref[column(*tables, row, r, spare)] for r in range(width)], axis=1
    )
    product = lax.dot_general(
        left, tiles_ref[row], (((1,), (0,)), ((), ())), preferred_element_type=F32
    )
    return combine(product, coef, half)


def edge_row(values_ref, edge_ref, row, first, coef, half):
    width = edge_ref.shape[2]
    left = jnp.concatenate([values_ref[first + d] for d in range(width)], axis=1)
    right = jnp.concatenate(
        [
            jnp.concatenate([edge_ref[m, row, d].astype(BF16) for d in range(width)], axis=1)
            for m in range(2)
        ],
        axis=0,
    )
    product = lax.dot_general(left, right, NT, preferred_element_type=F32)
    return combine(product, coef, half)


def prepare_source(side, part, place, mix_ref, bias_ref, rate_ref, mixing_ref, own_ref, bias_out_ref, rate_out_ref):
    size = mix_ref.shape[0]
    mine = size // (side * side)
    at = lax.broadcasted_iota(jnp.int32, (size, size), 0)
    wanted = lax.broadcasted_iota(jnp.int32, (size, size), 1)
    outer, inner = at // (mine * side), lax.rem(at // mine, side)
    even = lax.rem(part, 2) == 0
    y = lax.rem(place // side + side - jnp.where(even, outer, inner), side)
    x = lax.rem(lax.rem(place, side) + side - jnp.where(even, inner, outer), side)
    chosen = (y * side + x) * mine + lax.rem(at, mine) == wanted
    pick = jnp.where(chosen, 1.0, 0.0).astype(BF16)
    mix = mix_ref[...]
    high = mix.astype(BF16)
    low = (mix - high.astype(F32)).astype(BF16)
    tiles = []
    for piece in (high, low):
        rows = lax.dot_general(
            pick, piece, (((1,), (0,)), ((), ())), preferred_element_type=F32
        ).astype(BF16)
        tiles.append(lax.dot_general(rows, pick, NT, preferred_element_type=F32))
    tile = jnp.concatenate(tiles, axis=0).astype(BF16)
    mixing_ref[...] = jnp.concatenate([tile, tile], axis=1)
    spare = jnp.zeros((TILE - 2 * mine, size), F32)
    tile = jnp.concatenate([tiles[0][:mine], tiles[1][:mine], spare], axis=0).astype(BF16)
    own_ref[...] = jnp.concatenate([tile, tile], axis=1)
    for source_ref, target_ref, scale in ((bias_ref, bias_out_ref, 1.0), (rate_ref, rate_out_ref, 0.5)):
        column = jnp.sum(jnp.where(chosen, source_ref[...], 0.0), axis=1, keepdims=True)
        target_ref[...] = jnp.broadcast_to(scale * column, target_ref.shape)


def exchanged(value):
    mine = value.shape[0] // (SIDE * SIDE)
    at = lambda a, b: (a * SIDE + b) * mine
    return jnp.concatenate(
        [value[at(b, a) : at(b, a) + mine] for a in range(SIDE) for b in range(SIDE)], axis=0
    )


def half_source(values, mixing, bias, rate):
    both = lax.dot_general(
        mixing, values, (((1,), (0,)), ((), ())), preferred_element_type=F32
    )
    half = bias.shape[0]
    inner = both[:half] + both[half : 2 * half] + bias
    return rate * inner * jnp.exp(-0.125 * inner * inner)


def edges_kernel(
    total, side, origin_ref, place_ref, cols_ref, count_ref, low_ref, high_ref,
    mix_ref, bias_ref, rate_ref,
    to_right_ref, to_left_ref, mixing_ref, own_ref, bias_out_ref, rate_out_ref,
):
    width, rows = cols_ref.shape
    for source_ref, target_ref, start in (
        (low_ref, to_right_ref, rows - REACH),
        (high_ref, to_left_ref, 0),
    ):
        for row in range(source_ref.shape[1]):
            n = start + row
            for d in range(width):
                wanted = origin_ref[0] * rows + n + d - REACH
                wanted = jnp.where(wanted < 0, wanted + total, wanted)
                wanted = jnp.where(wanted >= total, wanted - total, wanted)
                slot = jnp.int32(0)
                scale = jnp.float32(0.0)
                for r in range(width):
                    hit = jnp.logical_and(cols_ref[r, n] == wanted, r < count_ref[n])
                    slot = jnp.where(hit, r, slot)
                    scale = jnp.where(hit, 1.0, scale)
                for m in range(2):
                    target_ref[m, row, d] = source_ref[m, row, slot].astype(F32) * scale
    prepare_source(
        side, origin_ref[0], place_ref[0], mix_ref, bias_ref, rate_ref,
        mixing_ref, own_ref, bias_out_ref, rate_out_ref,
    )


def pack_edges(explicit_blocks, scalars, source, total, side):
    months, rows, width, block, _ = explicit_blocks.shape
    size = source[0].shape[0]
    spec = lambda count, at: pl.BlockSpec(
        (months, count, width, block, block), lambda i: (0, at, 0, 0, 0)
    )
    smem = pl.BlockSpec(memory_space=pltpu.SMEM)
    vmem = pl.BlockSpec(memory_space=pltpu.VMEM)
    shape = lambda count: jax.ShapeDtypeStruct((months, count, width, block, block), F32)
    return pl.pallas_call(
        functools.partial(edges_kernel, total, side),
        grid=(1,),
        in_specs=[smem] * 4
        + [spec(REACH, rows // REACH - 1), spec(REACH - 1, 0)]
        + [vmem] * 3,
        out_specs=[spec(REACH, 0), spec(REACH - 1, 0)] + [vmem] * 4,
        out_shape=[
            shape(REACH),
            shape(REACH - 1),
            jax.ShapeDtypeStruct((2 * size, 2 * size), BF16),
            jax.ShapeDtypeStruct((TILE, 2 * size), BF16),
            jax.ShapeDtypeStruct((size, block), F32),
            jax.ShapeDtypeStruct((size, block), F32),
        ],
        compiler_params=pltpu.CompilerParams(vmem_limit_bytes=56 * MIB),
        name="edges",
    )(*scalars, explicit_blocks, explicit_blocks, *source)


def load_kernel(
    explicit_ref, implicit_ref, tiles_ref, implicit_out_ref, explicit_here_ref, sems
):
    chunks = sems.shape[1]
    _, rows, width, block, _ = explicit_ref.shape
    step = rows // chunks
    copies = []
    for k, (source, target) in enumerate(
        ((explicit_ref, explicit_here_ref), (implicit_ref, implicit_out_ref))
    ):
        for c in range(chunks):
            at = pl.ds(c * step, step)
            copies.append(
                pltpu.make_async_copy(source.at[:, at], target.at[:, at], sems.at[k, c])
            )
    for copy in copies:
        copy.start()
    for row in range(rows):
        if row % step == 0:
            copies[row // step].wait()
        for r in range(0, width, 2):
            both = jnp.concatenate(
                [
                    jnp.concatenate([explicit_here_ref[m, row, r + k] for k in range(2)], axis=1)
                    for m in range(2)
                ],
                axis=0,
            )
            tiles_ref[row, r * block : (r + 2) * block, :] = both.T
    for copy in copies[chunks:]:
        copy.wait()


def load(explicit_blocks, implicit_blocks):
    months, rows, width, block, _ = explicit_blocks.shape
    hbm = pl.BlockSpec(memory_space=pl.ANY)
    vmem = pl.BlockSpec(memory_space=pltpu.VMEM)
    return pl.pallas_call(
        load_kernel,
        in_specs=[hbm, hbm],
        out_specs=[vmem, vmem],
        out_shape=[
            pltpu.VMEM((rows, width * block, months * block), explicit_blocks.dtype),
            pltpu.VMEM(implicit_blocks.shape, implicit_blocks.dtype),
        ],
        scratch_shapes=[
            pltpu.VMEM(explicit_blocks.shape, explicit_blocks.dtype),
            pltpu.SemaphoreType.DMA((2, 6)),
        ],
        compiler_params=pltpu.CompilerParams(vmem_limit_bytes=44 * MIB),
        cost_estimate=pl.CostEstimate(flops=0, bytes_accessed=24 * MIB, transcendentals=0),
        name="load",
    )(explicit_blocks, implicit_blocks)


def first_kernel(
    total, origin_ref, cols_ref, count_ref, month_ref, weight_ref, explicit_ref, implicit_ref,
    near_ref, next_ref, far_ref, back_ref, left_ref, right_ref, mixing_ref, bias_ref, rate_ref,
    low_ref, high_ref, middle_ref, values_ref,
):
    coef = coefficients(month_ref, weight_ref, 0)
    tables = (total, origin_ref, cols_ref, count_ref)
    rows = implicit_ref.shape[1]
    block = implicit_ref.shape[-1]
    tracers = bias_ref.shape[0]
    ext = rows + LOW + HIGH
    share = near_ref.shape[0] // ext
    zero = jnp.zeros((2 * tracers, block), BF16)
    values_ref[ext] = zero
    middle_ref[ext - REACH] = zero
    for b in range(ext):
        parts = [
            ref[pl.ds(b, share, stride=ext), :] for ref in (near_ref, next_ref, far_ref, back_ref)
        ]
        split_store(values_ref, b, jnp.concatenate(parts, axis=0))
    mixing, bias, rate = mixing_ref[...], bias_ref[...], rate_ref[...]

    def finish(frame, product):
        source = half_source(values_ref[frame + REACH], mixing, bias, rate)
        split_store(middle_ref, frame, product + source)

    for row in range(REACH):
        finish(row, edge_row(values_ref, left_ref, row, row, coef, tracers))
    for row in range(REACH - 1):
        frame = rows + REACH + row
        finish(frame, edge_row(values_ref, right_ref, row, frame, coef, tracers))
    for row in range(rows):
        finish(row + REACH, tile_row(values_ref, explicit_ref, tables, row, coef, tracers))
    for at in range(LOW):
        low_ref[:, at * block : (at + 1) * block] = own_row(
            middle_ref, implicit_ref, tables, rows - LOW + at, REACH, coef, tracers
        )
    for row in range(HIGH):
        high_ref[:, row * block : (row + 1) * block] = own_row(
            middle_ref, implicit_ref, tables, row, REACH, coef, tracers
        )


def inner_kernel(
    total, origin_ref, cols_ref, count_ref, month_ref, weight_ref, explicit_ref, implicit_ref,
    low_ref, high_ref, middle_ref, mixing_ref, bias_ref, rate_ref,
    field_ref, own_ref, own_middle_ref,
):
    coef = coefficients(month_ref, weight_ref, 0)
    tables = (total, origin_ref, cols_ref, count_ref)
    rows = implicit_ref.shape[1]
    block = implicit_ref.shape[-1]
    tracers = low_ref.shape[0]
    mine = bias_ref.shape[0] // (SIDE * SIDE)
    ext = rows + LOW + HIGH

    def put(row, result):
        split_store(field_ref, row, result)
        own_store(own_ref, row + LOW, result[:mine])

    for at in range(LOW):
        put(rows - LOW + at, low_ref[:, at * block : (at + 1) * block])
    for row in range(HIGH):
        put(row, high_ref[:, row * block : (row + 1) * block])
    for row in range(HIGH, rows - LOW):
        put(row, own_row(middle_ref, implicit_ref, tables, row, REACH, coef, tracers))
    own_ref[ext] = jnp.zeros((TILE, block), BF16)
    coef = coefficients(month_ref, weight_ref, 1)
    mixing, bias, rate = mixing_ref[...], bias_ref[:mine, :], rate_ref[:mine, :]
    for row in range(REACH, rows - REACH + 1):
        product = tile_row(own_ref, explicit_ref, tables, row, coef, mine)
        source = half_source(field_ref[row], mixing, bias, rate)
        own_store(own_middle_ref, row + REACH, product + source)


def last_kernel(
    total, origin_ref, cols_ref, count_ref, month_ref, weight_ref, low_in_ref, high_in_ref,
    field_ref, own_in_ref, own_middle_in_ref, explicit_ref, implicit_ref, left_ref, right_ref,
    mixing_ref, bias_ref, rate_ref, out_ref, halo_ref, own_ref, own_middle_ref,
):
    coef = coefficients(month_ref, weight_ref, 1)
    tables = (total, origin_ref, cols_ref, count_ref)
    rows = implicit_ref.shape[1]
    block = implicit_ref.shape[-1]
    mine = bias_ref.shape[0] // (SIDE * SIDE)
    ext = rows + LOW + HIGH
    own_ref[LOW : LOW + rows] = own_in_ref[LOW : LOW + rows]
    own_ref[ext] = jnp.zeros((TILE, block), BF16)
    own_middle_ref[2 * REACH : rows + 1] = own_middle_in_ref[2 * REACH : rows + 1]
    own_middle_ref[ext - REACH] = jnp.zeros((TILE, block), BF16)
    for b in range(LOW + HIGH):
        if b < LOW:
            value, frame = low_in_ref[:, b * block : (b + 1) * block], b
        else:
            value, frame = high_in_ref[:, (b - LOW) * block : (b - LOW + 1) * block], rows + b
        value = exchanged(value)
        split_store(halo_ref, b, value)
        own_store(own_ref, frame, value[:mine])
    mixing, bias, rate = mixing_ref[...], bias_ref[:mine, :], rate_ref[:mine, :]

    def finish(frame, values, product):
        own_store(own_middle_ref, frame, product + half_source(values, mixing, bias, rate))

    for row in range(REACH):
        product = edge_row(own_ref, left_ref, row, row, coef, mine)
        finish(row, halo_ref[row + REACH], product)
    for row in range(REACH - 1):
        frame = rows + REACH + row
        product = edge_row(own_ref, right_ref, row, frame, coef, mine)
        finish(frame, halo_ref[LOW + row], product)
    for row in [*range(REACH), *range(rows - REACH + 1, rows)]:
        product = tile_row(own_ref, explicit_ref, tables, row, coef, mine)
        finish(row + REACH, field_ref[row], product)
    for row in range(rows):
        out_ref[:, row * block : (row + 1) * block] = own_row(
            own_middle_ref, implicit_ref, tables, row, REACH, coef, mine
        )


def call(kernel, name, smem_count, hbm_count, args, outs, scratch, flops, limit):
    smem = pl.BlockSpec(memory_space=pltpu.SMEM)
    vmem = pl.BlockSpec(memory_space=pltpu.VMEM)
    hbm = pl.BlockSpec(memory_space=pltpu.HBM)
    return pl.pallas_call(
        kernel,
        in_specs=[smem] * smem_count
        + [hbm] * hbm_count
        + [vmem] * (len(args) - smem_count - hbm_count),
        out_specs=[vmem] * len(outs),
        out_shape=outs,
        scratch_shapes=scratch,
        compiler_params=pltpu.CompilerParams(vmem_limit_bytes=limit * MIB),
        cost_estimate=pl.CostEstimate(flops=flops, bytes_accessed=8 * MIB, transcendentals=0),
        name=name,
    )(*args)


def per_device(
    tracers,
    explicit_blocks,
    implicit_blocks,
    column_blocks,
    block_count,
    month_pair,
    weight_num,
    source_mix,
    source_bias,
    source_rate,
):
    rows, width = column_blocks.shape
    block = explicit_blocks.shape[-1]
    parts = lax.axis_size("pts")
    groups = lax.axis_size("trc")
    mine = tracers.shape[0]
    total = source_mix.shape[0]
    ext = rows + LOW + HIGH
    forward = [(i, (i + 1) % parts) for i in range(parts)]
    backward = [(target, source) for source, target in forward]

    low = lax.ppermute(tracers, "pts", forward)[:, -LOW * block :]
    high = lax.ppermute(tracers, "pts", backward)[:, : HIGH * block]
    origin = lax.axis_index("pts").astype(jnp.int32).reshape(1)
    place = lax.axis_index("trc").astype(jnp.int32).reshape(1)
    scalars = (origin, column_blocks.T, block_count, month_pair, weight_num)
    to_right, to_left, *source = pack_edges(
        explicit_blocks,
        (origin, place, column_blocks.T, block_count),
        (source_mix, source_bias[None], source_rate[None]),
        rows * parts,
        SIDE,
    )
    low, high, to_right, to_left = lax.optimization_barrier((low, high, to_right, to_left))
    extended = jnp.concatenate([low, tracers, high], axis=1).reshape(mine * ext, block)
    both = ("pts", "trc")

    def along(stage, k):
        moves = []
        for p in range(parts):
            for t in range(groups):
                y, x = divmod(t, SIDE)
                if (p + stage) % 2 == 0:
                    source_at = y * SIDE + (x - k) % SIDE
                else:
                    source_at = (y - k) % SIDE * SIDE + x
                moves.append((p * groups + source_at, p * groups + t))
        return moves

    line = jnp.concatenate(
        [extended] + [lax.ppermute(extended, both, along(0, k)) for k in range(1, SIDE)]
    )
    line, explicit_blocks, implicit_blocks = lax.optimization_barrier(
        (line, explicit_blocks, implicit_blocks)
    )
    gathered = [line] + [lax.ppermute(line, both, along(1, k)) for k in range(1, SIDE)]
    explicit_blocks, implicit_blocks = load(explicit_blocks, implicit_blocks)
    left = lax.ppermute(to_right, "pts", forward)
    right = lax.ppermute(to_left, "pts", backward)

    shape = jax.ShapeDtypeStruct
    stack = lambda count: pltpu.VMEM((count, 2 * total, block), BF16)
    one = 2 * 2 * total * 2 * block * width * block
    own = lambda count: shape((count, TILE, block), BF16)
    mixing, own_mixing, bias, rate = source
    own_source = (own_mixing, bias, rate)
    low, high, middle = call(
        functools.partial(first_kernel, rows * parts), "first", 5, 0,
        (
            *scalars, explicit_blocks, implicit_blocks, *gathered, left, right,
            mixing, bias, rate,
        ),
        [
            shape((total, LOW * block), F32),
            shape((total, HIGH * block), F32),
            shape((ext - REACH + 1, 2 * total, block), BF16),
        ],
        [stack(ext + 1)],
        33 * one, 12,
    )
    low_in = lax.ppermute(low, "pts", forward)
    high_in = lax.ppermute(high, "pts", backward)
    field, own_field, own_middle = call(
        functools.partial(inner_kernel, rows * parts), "inner", 5, 0,
        (*scalars, explicit_blocks, implicit_blocks, low, high, middle, *own_source),
        [shape((rows, 2 * total, block), BF16), own(ext + 1), own(ext - REACH + 1)],
        [],
        39 * one, 12,
    )
    (advanced,) = call(
        functools.partial(last_kernel, rows * parts), "last", 5, 0,
        (
            *scalars, low_in, high_in, field, own_field, own_middle,
            explicit_blocks, implicit_blocks, left, right, *own_source,
        ),
        [shape((mine, rows * block), F32)],
        [
            stack(LOW + HIGH),
            pltpu.VMEM((ext + 1, TILE, block), BF16),
            pltpu.VMEM((ext - REACH + 1, TILE, block), BF16),
        ],
        30 * one, 12,
    )
    return advanced


def solution(mesh):
    in_specs = (
        P("trc", "pts"),
        P(None, "pts", None, None, None),
        P(None, "pts", None, None, None),
        P("pts", None),
        P("pts"),
        P(),
        P(),
        P(),
        P(),
        P(),
    )
    out_specs = P("trc", "pts")
    return jax.shard_map(
        per_device, mesh=mesh, in_specs=in_specs, out_specs=out_specs, check_vma=False
    )
```
